128 devices in a mesh: req: 8 (over y, core), sp: 16 (over z, x).
Axes of the slice: x: 4, y: 4, z: 4, core: 2. Of those that a mesh axis runs over, the one named last changes fastest.
Arguments:
- hidden: bfloat16 [8, 4096, 3072], P('req', 'sp'), may hold values from -6 to 6
- latent_query_key_value: bfloat16 [8, 4096, 3, 2048], P('req', 'sp'), may hold values from -6 to 6
- features: bfloat16 [64, 128, 1152], P('req', 'sp'), may hold values from -6 to 6
- image_request: int32 [64, 1], P('req'), may hold values from 0 to 7; in each aligned block of 8 rows (0 to 7, 8 to 15, ...) at most 2 rows name the same one
- image_key_weight: bfloat16 [1152, 2048], P(None, 'sp'), may hold values from -0.1875 to 0.1875
- image_value_weight: bfloat16 [1152, 2048], P(None, 'sp'), may hold values from -0.1875 to 0.1875
- caller_lowfactor_index: int32 [8], replicated, may hold values from 0 to 15
- request_rank: int32 [8], replicated, may hold values from 16 to 64
- lowfactor_reducing_matrix: bfloat16 [16, 3072, 64], P('req'), may hold values from -0.109375 to 0.109375
- lowfactor_expanding_matrix: bfloat16 [16, 64, 2048], P('req'), may hold values from -0.75 to 0.75
Outputs:
- attended: bfloat16 [8, 4096, 2048], P('req', 'sp')
The draws below stay inside these ranges and needn't reach their ends.
Inputs may be any that keep to these rules, and one draw needn't show every extreme that they name: `image_request`: in each block of 8 images of one index of req, at most 2 belong to one request; every request owns at least one image.
All inputs are finite; a program needn't handle non-finite values.
Results may differ from the reference program's by a relative error of at most 0.0093.
Values may be sent and summed in bfloat16 or wider, within the bound.
No kernel may reach another device: no remote copies, remote signals or barrier semaphores. Data moves between devices by JAX's collectives and lax.ppermute only.
A program may use at most 128 MiB of HBM per device.

```python
import math
import jax
import jax.numpy as jnp
import numpy as np
from jax import lax

EMBED_SPAN = 3072
E = 1152
HEADS = 16
HD = 128
PER_HEAD_SPAN = 2048
SEQ = 4096
CALLER_COUNT = 8
IMG_TOK = 128
IMG_DEV = 8
IMAGES = 64
CAP = 2
TOP_INNER_SPAN = 64
LOWFACTOR_COUNT = 16
N_REQ = 8


def draw_latent_query_key_value(key, part):
    key = jax.random.fold_in(key, 11)
    key_base = jax.random.fold_in(key, 0)
    array_shape = (CALLER_COUNT, SEQ // 64, 64, 3, PER_HEAD_SPAN)
    values = jnp.clip(jax.random.normal(key_base, array_shape, jnp.float32), -6.0, 6.0)
    return values.reshape(CALLER_COUNT, SEQ, 3, PER_HEAD_SPAN).astype(jnp.bfloat16)


def with_ends(array, key, least, top_value):
    longest = array.shape.index(max(array.shape))
    spots = []
    for shift in (0, 1):
        where = [jax.random.randint(jax.random.fold_in(key, axis), (), 0, length) for axis, length in enumerate(array.shape)]
        where[longest] = (where[longest] + shift) % array.shape[longest]
        spots.append(tuple(where))
    return array.at[spots[0]].set(least).at[spots[1]].set(top_value)


def steps_of(key, dims, cuts, least, top_value):
    def one(axis_at, parts):
        draws = jax.random.uniform(jax.random.fold_in(jax.random.fold_in(key, 6), axis_at), (parts,), jnp.float32, least / len(cuts), top_value / len(cuts))
        return jnp.repeat(jnp.exp(draws), dims[axis_at] // parts).reshape((-1,) + (1,) * (len(dims) - axis_at - 1))

    loudness = one(*cuts[0])
    for cut in cuts[1:]:
        loudness = loudness * one(*cut)
    return loudness


def routed_block(rng, own, number, rows, amount, top, limit, skew):
    ranking = jax.random.permutation(rng, amount)
    heavy_load, usual = load_shares(amount, rows * top, limit, skew, True), load_shares(amount, rows * top, limit, skew, False)
    places = jnp.arange(amount)

    def named(lengths, turn):
        used = int((lengths > 0).sum())
        fixed = max(1, used // 4)
        passed = fixed + (places - fixed + turn * (used - fixed)) % max(1, amount - fixed)
        return jnp.zeros((amount,), jnp.int32).at[ranking[jnp.where(places < fixed, places, passed)]].set(jnp.asarray(lengths, jnp.int32))

    lengths = jnp.where(number % 4 == 0, named(heavy_load, number // 4), named(usual, number - number // 4 - 1))
    mixed = jax.random.permutation(jax.random.fold_in(own, 3), amount)
    source_of, receiver = mixed[0:amount // 2 * 2:2], mixed[1:amount // 2 * 2:2]
    slack = jnp.minimum(lengths[source_of] - 1, limit - lengths[receiver]) // 2
    slack = jnp.where((source_of == ranking[0]) | (receiver == ranking[0]) | (lengths[receiver] == 0), 0, jnp.maximum(slack, 0))
    passed = jax.random.randint(jax.random.fold_in(own, 4), (amount // 2,), 0, 1 << 20) % (slack + 1)
    lengths = lengths.at[source_of].add(-passed).at[receiver].add(passed)
    labels = jnp.searchsorted(jnp.cumsum(lengths), jnp.arange(rows * top), side="right").astype(jnp.int32)
    table = labels.reshape(top, rows).T
    table = table[jax.random.permutation(jax.random.fold_in(own, 1), rows)]
    turn = jax.random.randint(jax.random.fold_in(own, 2), (rows, 1), 0, top)
    return jnp.take_along_axis(table, (jnp.arange(top)[None, :] + turn) % top, axis=1)


def load_shares(number_of, total, limit, lean, full):
    portions = [(1 << 20) // math.isqrt(grade ** lean) + 1 for grade in range(1, number_of + 1)]
    largest = limit if full else min(limit, max(-(-total // number_of), total * portions[0] // sum(portions)))
    least = 1 if total - largest >= number_of - 1 else 0
    holding, surplus = [largest] + [least] * (number_of - 1), total - largest - least * (number_of - 1)
    while surplus > 0:
        candidates = [i for i in range(1, number_of) if holding[i] < largest] or [i for i in range(1, number_of) if holding[i] < limit]
        pool, remaining = sum([portions[i] for i in candidates]), surplus
        for i in candidates:
            addition = min(limit - holding[i], max(1, remaining * portions[i] // pool), surplus)
            holding[i] = holding[i] + addition
            surplus = surplus - addition
    return np.array(holding)


def scatter_about(key, extent, deviation, most, pieces=(), dtype=jnp.bfloat16):
    loudness = steps_of(key, extent, pieces, -0.22, 0.18) if pieces else 1.0
    entries = jax.random.normal(key, extent, jnp.float32) * deviation * loudness
    return jnp.minimum(jnp.maximum(entries, -most), most).astype(dtype)


def setup_inputs(seed: int = 0) -> dict:
    arg_keys = jax.random.split(jax.random.key(seed), 11)
    hidden = scatter_about(arg_keys[0], (CALLER_COUNT, SEQ, EMBED_SPAN), 1.0, 6.0, ((0, 8), (1, 16)))
    latent_query_key_value = draw_latent_query_key_value(jax.random.fold_in(arg_keys[10], 71), 0)
    features = scatter_about(arg_keys[2], (IMAGES, IMG_TOK, E), 1.0, 6.0, ((0, 8), (1, 16)))
    image_request_keys = jax.random.split(jax.random.fold_in(arg_keys[3], 1), IMAGES // IMG_DEV)
    image_request_turns = jax.random.permutation(jax.random.fold_in(arg_keys[3], 3), IMAGES // IMG_DEV)
    image_request = jax.vmap(lambda own, number: routed_block(jax.random.fold_in(arg_keys[3], 2), own, number, IMG_DEV, CALLER_COUNT, 1, CAP, 2))(image_request_keys, image_request_turns).reshape((IMAGES, 1))
    image_key_weight = scatter_about(arg_keys[4], (E, PER_HEAD_SPAN), E ** -0.5, 0.1875, ((1, 16),))
    image_value_weight = scatter_about(arg_keys[5], (E, PER_HEAD_SPAN), E ** -0.5, 0.1875, ((1, 16),))
    caller_lowfactor_index = with_ends(jax.random.randint(arg_keys[6], (CALLER_COUNT,), 0, LOWFACTOR_COUNT), jax.random.fold_in(arg_keys[6], 1), 0, LOWFACTOR_COUNT - 1).astype(jnp.int32)
    request_rank = with_ends(jax.random.randint(arg_keys[7], (CALLER_COUNT,), TOP_INNER_SPAN // 4, TOP_INNER_SPAN + 1), jax.random.fold_in(arg_keys[7], 1), TOP_INNER_SPAN // 4, TOP_INNER_SPAN).astype(jnp.int32)
    lowfactor_reducing_matrix = scatter_about(arg_keys[8], (LOWFACTOR_COUNT, EMBED_SPAN, TOP_INNER_SPAN), EMBED_SPAN ** -0.5, 0.109375, ((0, 8),))
    lowfactor_expanding_matrix = scatter_about(arg_keys[9], (LOWFACTOR_COUNT, TOP_INNER_SPAN, PER_HEAD_SPAN), TOP_INNER_SPAN ** -0.5, 0.75, ((0, 8),))
    return {"hidden": hidden, "latent_query_key_value": latent_query_key_value, "features": features, "image_request": image_request, "image_key_weight": image_key_weight, "image_value_weight": image_value_weight, "caller_lowfactor_index": caller_lowfactor_index, "request_rank": request_rank, "lowfactor_reducing_matrix": lowfactor_reducing_matrix, "lowfactor_expanding_matrix": lowfactor_expanding_matrix}


adapter_alpha = 16.0
ip_scale = 1.0


def attend(query_row_block, key_rows, value_rows, key_valid):
    scores = jnp.dot(query_row_block, key_rows.T, preferred_element_type=jnp.float32) * (HD ** -0.5)
    scores = jnp.where(key_valid[None, :], scores, -1e30)
    row_max = jnp.max(scores, axis=-1, keepdims=True)
    weights = jnp.exp(scores - row_max)
    weights = (weights / jnp.sum(weights, axis=-1, keepdims=True)).astype(jnp.bfloat16)
    return jnp.dot(weights, value_rows, preferred_element_type=jnp.float32)


def reference(hidden, latent_query_key_value, features, image_request, image_key_weight, image_value_weight, caller_lowfactor_index, request_rank, lowfactor_reducing_matrix, lowfactor_expanding_matrix):
    def one_request(request_number):
        adapter_choice = caller_lowfactor_index[request_number]
        adapter_rank_value = request_rank[request_number]
        rank_activations = jnp.dot(hidden[request_number], lowfactor_reducing_matrix[adapter_choice], preferred_element_type=jnp.float32)
        rank_activations = jnp.where(jnp.arange(TOP_INNER_SPAN)[None, :] < adapter_rank_value, rank_activations, 0.0).astype(jnp.bfloat16)
        query_update = jnp.dot(rank_activations, lowfactor_expanding_matrix[adapter_choice], preferred_element_type=jnp.float32)
        query_row_block = (latent_query_key_value[request_number, :, 0].astype(jnp.float32) + (adapter_alpha / adapter_rank_value.astype(jnp.float32)) * query_update).astype(jnp.bfloat16)
        owners = image_request[:, 0]
        image_order = jnp.argsort((owners != request_number).astype(jnp.int32), stable=True)[:N_REQ * CAP]
        slot_valid = owners[image_order] == request_number
        flat_rows = features[image_order].reshape(-1, E)
        img_keys = jnp.dot(flat_rows, image_key_weight, preferred_element_type=jnp.float32).astype(jnp.bfloat16)
        img_vals = jnp.dot(flat_rows, image_value_weight, preferred_element_type=jnp.float32).astype(jnp.bfloat16)
        token_valid = jnp.repeat(slot_valid, IMG_TOK)
        all_valid = jnp.ones((SEQ,), bool)

        def per_head(head):
            start = (head * HD).astype(jnp.int32)
            pick = lambda arr: lax.dynamic_slice_in_dim(arr, start, HD, 1)
            own = attend(pick(query_row_block), pick(latent_query_key_value[request_number, :, 1]), pick(latent_query_key_value[request_number, :, 2]), all_valid)
            image = attend(pick(query_row_block), pick(img_keys), pick(img_vals), token_valid)
            return (own + ip_scale * image).astype(jnp.bfloat16)

        per_heads = lax.map(per_head, jnp.arange(HEADS).astype(jnp.int32))
        return jnp.transpose(per_heads, (1, 0, 2)).reshape(SEQ, PER_HEAD_SPAN)

    return lax.map(one_request, jnp.arange(CALLER_COUNT).astype(jnp.int32))
```

```python
import functools

import numpy as np

import jax
import jax.numpy as jnp
from jax import lax
from jax.experimental import pallas as pl
from jax.experimental.pallas import tpu as pltpu
from jax.sharding import PartitionSpec as P

HD = 128
CAP = 2
TOK = 256
HEADS = 16
GROUPS = 8
SLOTS = GROUPS * CAP
IMG_TOK = 128
ENC = 1152
RANK = 64
WIDTH = 3072
FLAG_ROWS = 16
IMG_SOURCES = 4
PACKED = 3 * TOK + 2 * RANK

adapter_alpha = 16.0
ip_scale = 1.0

SCALE2 = float(np.log2(np.e) / np.sqrt(HD))
LEAST_TOTAL, LARGEST_TOTAL = 2.0**-80, 2.0**96

bf16 = jnp.bfloat16
f32 = jnp.float32
NT = (((1,), (1,)), ((), ()))
TN = (((0,), (0,)), ((), ()))


SMEM = pl.BlockSpec(memory_space=pltpu.SMEM)


def adapter_at(here_ref, index_ref):
    return (here_ref[0] // 2 - index_ref[here_ref[0]] // 4 + 4) % 4


def params(mib):
    return pltpu.CompilerParams(vmem_limit_bytes=mib << 20)


def moving(nbytes):
    return pl.CostEstimate(flops=0, bytes_accessed=nbytes, transcendentals=0)


def pack_kernel(k_ref, v_ref, q_ref, o_ref):
    for h in range(HEADS):
        for p, x_ref in enumerate((k_ref, v_ref, q_ref)):
            o_ref[h, p * TOK : (p + 1) * TOK] = x_ref[0, :, h * HD : (h + 1) * HD]


def pack_heads(planes):
    def plane(p):
        return pl.BlockSpec((1, TOK, HEADS * HD), lambda i: (p, 0, 0))

    return pl.pallas_call(
        pack_kernel,
        grid=(1,),
        in_specs=[plane(1), plane(2), plane(0)],
        out_specs=pl.BlockSpec((HEADS, 3 * TOK, HD), lambda i: (0, 0, 0)),
        out_shape=jax.ShapeDtypeStruct((HEADS, PACKED, HD), bf16),
        compiler_params=params(24),
        cost_estimate=moving(6 << 20),
    )(planes, planes, planes)


def choose_kernel(here_ref, index_ref, own_ref, other_ref, *o_refs):
    y, core = here_ref[0] // 2, here_ref[0] % 2
    for k in range(4):
        local = index_ref[(y + k) % 4 * 2 + core] % 4

        @pl.when(local // 2 == core)
        def _():
            o_refs[k][...] = own_ref[local % 2]

        @pl.when(local // 2 != core)
        def _():
            o_refs[k][...] = other_ref[local % 2]


def choose_adapters(here, index, own, other):
    vmem = pl.BlockSpec(memory_space=pltpu.VMEM)
    one = jax.ShapeDtypeStruct(own.shape[1:], bf16)
    return pl.pallas_call(
        choose_kernel,
        in_specs=[SMEM, SMEM, vmem, vmem],
        out_specs=[vmem] * 4,
        out_shape=[one] * 4,
        compiler_params=params(24),
        cost_estimate=moving(own.size * 8),
    )(here, index, own, other)


def rank_kernel(here_ref, index_ref, rank_ref, hidden_ref, a0, a1, a2, a3, _, o_ref, acts_ref, sems):
    def emit(a_ref):
        acts = lax.dot_general(a_ref[...], hidden_ref[...], NT, preferred_element_type=f32)
        kept = lax.broadcasted_iota(jnp.int32, acts.shape, 0) < rank_ref[here_ref[0]]
        acts = jnp.where(kept, acts, 0.0).astype(bf16)
        acts_ref[:RANK] = acts[:, :HD]
        acts_ref[RANK:] = acts[:, HD:]

    chosen = adapter_at(here_ref, index_ref)
    for j, a_ref in enumerate((a0, a1, a2, a3)):
        pl.when(chosen == j)(functools.partial(emit, a_ref))
    copies = [
        pltpu.make_async_copy(acts_ref, o_ref.at[h, pl.ds(3 * TOK, 2 * RANK)], sems.at[h])
        for h in range(HEADS)
    ]
    for copy in copies:
        copy.start()
    for copy in copies:
        copy.wait()


def add_ranks(here, index, rank, hidden, adapters, packed):
    down = pl.BlockSpec((RANK, WIDTH), lambda i: (0, 0))
    hbm = pl.BlockSpec(memory_space=pl.ANY)
    return pl.pallas_call(
        rank_kernel,
        grid=(1,),
        in_specs=[SMEM, SMEM, SMEM, pl.BlockSpec((TOK, WIDTH), lambda i: (0, 0))] + [down] * 4 + [hbm],
        out_specs=hbm,
        out_shape=jax.ShapeDtypeStruct(packed.shape, bf16),
        scratch_shapes=[pltpu.VMEM((2 * RANK, HD), bf16), pltpu.SemaphoreType.DMA((HEADS,))],
        input_output_aliases={8: 0},
        compiler_params=params(32),
        cost_estimate=pl.CostEstimate(
            flops=2 * TOK * WIDTH * RANK, bytes_accessed=4 << 20, transcendentals=0
        ),
    )(here, index, rank, hidden, *adapters, packed)


def image_kernel(here_ref, owner_ref, f_ref, wk_ref, wv_ref, *refs):
    outs, kv = refs[:GROUPS], refs[GROUPS]
    step = pl.program_id(0)
    weights = jnp.concatenate([wk_ref[...], wv_ref[...]], axis=1)
    rows = f_ref[...].reshape(IMG_SOURCES * 64, ENC)
    rows = jnp.dot(rows, weights, preferred_element_type=f32).reshape(IMG_SOURCES, 8, 8, 2 * HD)
    per_step = IMG_SOURCES * 8
    for i in range(8):
        kv[i, pl.ds(pl.multiple_of(step * per_step, per_step), per_step)] = rows[:, i].reshape(
            per_step, 2 * HD
        )

    @pl.when(step == pl.num_programs(0) - 1)
    def _():
        y, core = here_ref[0] // 2, here_ref[0] % 2
        for t in range(GROUPS):
            target = (y + t // 2) % 4 * 2 + (core + t % 2) % 2
            seen, held = jnp.int32(0), [jnp.int32(-1), jnp.int32(-1)]
            for i in range(8):
                hit = owner_ref[i] == target
                held = [jnp.where(hit & (seen == c), i, held[c]) for c in range(CAP)]
                seen = seen + hit.astype(jnp.int32)
            for c in range(CAP):
                got = kv[jnp.maximum(held[c], 0)]
                outs[t][c * IMG_TOK : (c + 1) * IMG_TOK] = jnp.where(held[c] >= 0, got, 0.0).astype(bf16)
            row = lax.broadcasted_iota(jnp.int32, (FLAG_ROWS, 2 * HD), 0)
            both = jnp.where(row == 0, held[0], held[1])
            outs[t][CAP * IMG_TOK :] = jnp.where(both >= 0, 1.0, 0.0).astype(bf16)


def place_images(here, owners, gathered, wk, wv):
    rows = CAP * IMG_TOK + FLAG_ROWS
    whole = pl.BlockSpec((ENC, HD), lambda i: (0, 0))
    return pl.pallas_call(
        image_kernel,
        grid=(HEADS // IMG_SOURCES,),
        in_specs=[SMEM, SMEM, pl.BlockSpec((IMG_SOURCES, 64, ENC), lambda i: (i, 0, 0)), whole, whole],
        out_specs=[pl.BlockSpec((rows, 2 * HD), lambda i: (0, 0))] * GROUPS,
        out_shape=[jax.ShapeDtypeStruct((rows, 2 * HD), bf16)] * GROUPS,
        scratch_shapes=[pltpu.VMEM((8, IMG_TOK, 2 * HD), f32)],
        compiler_params=params(60),
        cost_estimate=pl.CostEstimate(
            flops=2 * 1024 * ENC * 2 * HD, bytes_accessed=5 << 20, transcendentals=0
        ),
    )(here, owners, gathered, wk, wv)


def unpack_kernel(x_ref, o_ref):
    for h in range(HEADS):
        o_ref[0, :, h * HD : (h + 1) * HD] = x_ref[h]


def unpack_heads(per_head):
    rows = 128
    return pl.pallas_call(
        unpack_kernel,
        grid=(TOK // rows,),
        in_specs=[pl.BlockSpec((HEADS, rows, HD), lambda i: (0, i, 0))],
        out_specs=pl.BlockSpec((1, rows, HEADS * HD), lambda i: (0, i, 0)),
        out_shape=jax.ShapeDtypeStruct((1, TOK, HEADS * HD), bf16),
        compiler_params=pltpu.CompilerParams(vmem_limit_bytes=24 << 20),
        cost_estimate=pl.CostEstimate(flops=0, bytes_accessed=TOK * HEADS * HD * 4, transcendentals=0),
    )(per_head)


def attend_kernel(here_ref, index_ref, rank_ref, q_ref, acts_ref, kv_ref, u0, u1, u2, u3, *refs, per_step, chunk):
    images, (o_ref, q_s) = refs[:GROUPS], refs[GROUPS:]
    rows = per_step * TOK
    keys = HEADS * TOK
    blocks = chunk // TOK
    pairs = chunk // (CAP * IMG_TOK)
    img_chunks = SLOTS * IMG_TOK // chunk

    def own_key(c):
        return kv_ref[pl.ds(c * blocks, blocks), :TOK].reshape(chunk, HD)

    def own_val(c):
        return kv_ref[pl.ds(c * blocks, blocks), TOK:].reshape(chunk, HD)

    def img_part(c, low):
        return jnp.concatenate(
            [images[c * pairs + i][: CAP * IMG_TOK, low : low + HD] for i in range(pairs)], axis=0
        )

    def flag(s):
        rows16 = images[s // CAP][CAP * IMG_TOK :, :HD].astype(f32)
        return rows16[s % CAP : s % CAP + 1, :1] > 0.5

    chosen = adapter_at(here_ref, index_ref)
    rank = jnp.full((1, HD), rank_ref[here_ref[0]].astype(f32))
    scale = adapter_alpha / rank
    for j, up_ref in enumerate((u0, u1, u2, u3)):

        @pl.when(chosen == j)
        def _():
            up = up_ref[...]
            for i in range(per_step):
                for half in range(2):
                    acts = acts_ref[i, half * RANK : (half + 1) * RANK]
                    update = lax.dot_general(acts, up, TN, preferred_element_type=f32)
                    base = q_ref[i, half * HD : (half + 1) * HD].astype(f32)
                    q_s[i * TOK + half * HD : i * TOK + (half + 1) * HD] = (
                        base + scale * update
                    ).astype(bf16)

    q = q_s[...]

    def scores(key):
        return lax.dot_general(key, q, NT, preferred_element_type=f32) * SCALE2

    def finish(acc, total):
        return acc / jnp.sum(total, axis=0, keepdims=True)

    zeros = (jnp.zeros((HD, rows), f32), jnp.zeros((8, rows), f32))

    acc, own_total = zeros
    for c in range(keys // chunk):
        p = jnp.exp2(scores(own_key(c)))
        own_total = own_total + p.reshape(chunk // 8, 8, rows).sum(0)
        acc = acc + lax.dot_general(own_val(c), p.astype(bf16), TN, preferred_element_type=f32)
    own_total = jnp.sum(own_total, axis=0, keepdims=True)
    out = acc / own_total
    acc, img_total = zeros
    slots = chunk // IMG_TOK
    for c in range(img_chunks):
        p = jnp.exp2(scores(img_part(c, 0)))
        per_slot = p.reshape(slots, IMG_TOK // 8, 8, rows).sum(1)
        for s in range(slots):
            img_total = img_total + jnp.where(flag(c * slots + s), per_slot[s], 0.0)
        acc = acc + lax.dot_general(img_part(c, HD), p.astype(bf16), TN, preferred_element_type=f32)
    img_total = jnp.sum(img_total, axis=0, keepdims=True)
    out = out + ip_scale * (acc / img_total)
    o_ref[...] = out.T.astype(bf16).reshape(per_step, TOK, HD)
    low = jnp.min(jnp.minimum(own_total, img_total))
    high = jnp.max(jnp.maximum(own_total, img_total))
    in_range = (low >= LEAST_TOTAL) & (high <= LARGEST_TOTAL)

    @pl.when(jnp.logical_not(in_range))
    def _():
        def own_max(c, top):
            return jnp.maximum(top, scores(own_key(c)).reshape(chunk // 8, 8, rows).max(0))

        top = lax.fori_loop(0, keys // chunk, own_max, jnp.full((8, rows), -1e30, f32))
        top = jnp.max(top, axis=0, keepdims=True)

        def own_sum(c, carry):
            acc, total = carry
            p = jnp.exp2(scores(own_key(c)) - top)
            total = total + p.reshape(chunk // 8, 8, rows).sum(0)
            acc = acc + lax.dot_general(own_val(c), p.astype(bf16), TN, preferred_element_type=f32)
            return acc, total

        out = finish(*lax.fori_loop(0, keys // chunk, own_sum, zeros))

        def slot_scores(s):
            part = images[s // CAP][(s % CAP) * IMG_TOK : (s % CAP + 1) * IMG_TOK, :HD]
            return jnp.where(flag(s), scores(part), -1e30)

        top = jnp.full((8, rows), -1e30, f32)
        for s in range(SLOTS):
            top = jnp.maximum(top, slot_scores(s).reshape(IMG_TOK // 8, 8, rows).max(0))
        top = jnp.max(top, axis=0, keepdims=True)
        acc, total = zeros
        for s in range(SLOTS):
            p = jnp.exp2(slot_scores(s) - top)
            total = total + p.reshape(IMG_TOK // 8, 8, rows).sum(0)
            part = images[s // CAP][(s % CAP) * IMG_TOK : (s % CAP + 1) * IMG_TOK, HD:]
            acc = acc + lax.dot_general(part, p.astype(bf16), TN, preferred_element_type=f32)
        out = out + ip_scale * finish(acc, total)
        o_ref[...] = out.T.astype(bf16).reshape(per_step, TOK, HD)


def attend(here, index, rank, heads, adapters, images):
    per_step, chunk = 4, 512
    pairs = HEADS * TOK * (HEADS * TOK + SLOTS * IMG_TOK)
    up = pl.BlockSpec((RANK, HD), lambda i: (0, WIDTH // HD))
    image = pl.BlockSpec((CAP * IMG_TOK + FLAG_ROWS, 2 * HD), lambda i: (0, 0))
    return pl.pallas_call(
        functools.partial(attend_kernel, per_step=per_step, chunk=chunk),
        grid=(HEADS // per_step,),
        in_specs=[
            SMEM,
            SMEM,
            SMEM,
            pl.BlockSpec((per_step, TOK, HD), lambda i: (i, 2, 0)),
            pl.BlockSpec((per_step, 2 * RANK, HD), lambda i: (i, 3 * TOK // (2 * RANK), 0)),
            pl.BlockSpec((HEADS, 2 * TOK, HD), lambda i: (0, 0, 0)),
        ]
        + [up] * 4
        + [image] * GROUPS,
        out_specs=pl.BlockSpec((per_step, TOK, HD), lambda i: (i, 0, 0)),
        out_shape=jax.ShapeDtypeStruct((HEADS, TOK, HD), bf16),
        scratch_shapes=[pltpu.VMEM((per_step * TOK, HD), bf16)],
        compiler_params=params(60),
        cost_estimate=pl.CostEstimate(flops=pairs * HD * 4, bytes_accessed=6 << 20, transcendentals=pairs),
    )(here, index, rank, heads, heads, heads, *adapters, *images)


def along_req(k, d):
    return [(y * 2 + c, (y + k) % 4 * 2 + (c + d) % 2) for y in range(4) for c in range(2)]


def exchange(x):
    return lax.all_to_all(x, "sp", split_axis=0, concat_axis=0, tiled=True)


def after(x, *others):
    return lax.optimization_barrier((x,) + others)[0]


def shards(
    hidden,
    latent_query_key_value,
    features,
    image_request,
    image_key_weight,
    image_value_weight,
    caller_lowfactor_index,
    request_rank,
    lowfactor_reducing_matrix,
    lowfactor_expanding_matrix,
):
    here = lax.axis_index("req").reshape(1)
    place = lax.axis_index("sp").reshape(1)
    index, rank = caller_lowfactor_index, request_rank
    planes = latent_query_key_value[0].transpose(1, 0, 2)

    own = jnp.concatenate(
        [
            lowfactor_reducing_matrix.transpose(0, 2, 1),
            lax.dynamic_slice_in_dim(lowfactor_expanding_matrix, place[0] * HD, HD, 2),
        ],
        axis=2,
    )
    other = lax.ppermute(own, "req", along_req(0, 1))

    own_rows = after(features.reshape(64, ENC), own)
    gathered = exchange(jnp.broadcast_to(own_rows[None], (HEADS, 64, ENC)))

    chosen = choose_adapters(here, index, own, other)
    adapters = [chosen[0]] + [lax.ppermute(chosen[k], "req", along_req(k, 0)) for k in (1, 2, 3)]

    packed = add_ranks(here, index, rank, hidden[0], adapters, pack_heads(planes))
    heads = exchange(after(packed, gathered))

    ways = [(k, d) for k in range(4) for d in range(2)]
    placed = place_images(here, image_request[:, 0], gathered, image_key_weight, image_value_weight)
    images = [placed[0]] + [
        lax.ppermute(p, "req", along_req(k, d)) for p, (k, d) in zip(placed[1:], ways[1:])
    ]

    per_heads = attend(here, index, rank, heads, adapters, images)
    return unpack_heads(exchange(per_heads))


def solution(mesh):
    placed = (
        P("req", "sp", None),
        P("req", "sp", None, None),
        P("req", "sp", None),
        P("req", None),
        P(None, "sp"),
        P(None, "sp"),
        P(),
        P(),
        P("req", None, None),
        P("req", None, None),
    )
    return jax.shard_map(
        shards, mesh=mesh, in_specs=placed, out_specs=P("req", "sp", None), check_vma=False
    )
```

```python
import functools

import numpy as np

import jax
import jax.numpy as jnp
from jax import lax
from jax.experimental import pallas as pl
from jax.experimental.pallas import tpu as pltpu
from jax.sharding import PartitionSpec as P

HD = 128
CAP = 2
TOK = 256
HEADS = 16
GROUPS = 8
SLOTS = GROUPS * CAP
IMG_TOK = 128
ENC = 1152
RANK = 64
WIDTH = 3072
FLAG_ROWS = 16
HALF = TOK // 2
PACKED = 2 * TOK + 2 * RANK

adapter_alpha = 16.0
ip_scale = 1.0

SCALE2 = float(np.log2(np.e) / np.sqrt(HD))
LEAST_TOTAL, LARGEST_TOTAL = 2.0**-80, 2.0**96

bf16 = jnp.bfloat16
f32 = jnp.float32
NT = (((1,), (1,)), ((), ()))
TN = (((0,), (0,)), ((), ()))


SMEM = pl.BlockSpec(memory_space=pltpu.SMEM)


def params(mib):
    return pltpu.CompilerParams(vmem_limit_bytes=mib << 20)


def moving(nbytes):
    return pl.CostEstimate(flops=0, bytes_accessed=nbytes, transcendentals=0)


def pack_first_kernel(k_ref, v_ref, q_ref, o_ref):
    for h in range(HEADS):
        o_ref[h, :HALF] = k_ref[0, :, h * HD : (h + 1) * HD]
        o_ref[h, HALF:TOK] = v_ref[0, :, h * HD : (h + 1) * HD]
        o_ref[h, TOK:] = q_ref[0, :, h * HD : (h + 1) * HD]


def pack_second_kernel(k_ref, v_ref, o_ref):
    for h in range(HEADS):
        o_ref[h, :HALF] = k_ref[0, :, h * HD : (h + 1) * HD]
        o_ref[h, HALF:] = v_ref[0, :, h * HD : (h + 1) * HD]


def half_of(plane, part):
    return pl.BlockSpec((1, HALF, HEADS * HD), lambda i: (plane, part, 0))


def pack_first(planes):
    return pl.pallas_call(
        pack_first_kernel,
        grid=(1,),
        in_specs=[half_of(1, 0), half_of(2, 0), pl.BlockSpec((1, TOK, HEADS * HD), lambda i: (0, 0, 0))],
        out_specs=pl.BlockSpec((HEADS, 2 * TOK, HD), lambda i: (0, 0, 0)),
        out_shape=jax.ShapeDtypeStruct((HEADS, PACKED, HD), bf16),
        compiler_params=params(24),
        cost_estimate=moving(4 << 20),
    )(planes, planes, planes)


def pack_second(planes):
    return pl.pallas_call(
        pack_second_kernel,
        grid=(1,),
        in_specs=[half_of(1, 1), half_of(2, 1)],
        out_specs=pl.BlockSpec((HEADS, TOK, HD), lambda i: (0, 0, 0)),
        out_shape=jax.ShapeDtypeStruct((HEADS, TOK, HD), bf16),
        compiler_params=params(24),
        cost_estimate=moving(2 << 20),
    )(planes, planes)


def choose_kernel(here_ref, index_ref, own_ref, other_ref, o_ref):
    core = here_ref[0] % 2
    for y in range(4):
        local = index_ref[y * 2 + core] % 4

        @pl.when(local // 2 == core)
        def _():
            o_ref[y] = own_ref[local % 2]

        @pl.when(local // 2 != core)
        def _():
            o_ref[y] = other_ref[local % 2]


def choose_adapters(here, index, own, other):
    vmem = pl.BlockSpec(memory_space=pltpu.VMEM)
    return pl.pallas_call(
        choose_kernel,
        in_specs=[SMEM, SMEM, vmem, vmem],
        out_specs=vmem,
        out_shape=jax.ShapeDtypeStruct((4,) + own.shape[1:], bf16),
        compiler_params=params(24),
        cost_estimate=moving(own.size * 8),
    )(here, index, own, other)


def holder(here, index):
    return index[here[0]] // 4


def rank_kernel(here_ref, index_ref, rank_ref, hidden_ref, a_ref, _, o_ref, acts_ref, sems):
    acts = lax.dot_general(hidden_ref[...], a_ref[0], NT, preferred_element_type=f32)
    kept = lax.broadcasted_iota(jnp.int32, acts.shape, 1) < rank_ref[here_ref[0]]
    acts = jnp.where(kept, acts, 0.0)
    acts_ref[...] = jnp.concatenate([acts[:HALF], acts[HALF:]], axis=1).astype(bf16)
    copies = [
        pltpu.make_async_copy(acts_ref, o_ref.at[h, pl.ds(2 * TOK, 2 * RANK)], sems.at[h])
        for h in range(HEADS)
    ]
    for copy in copies:
        copy.start()
    for copy in copies:
        copy.wait()


def add_ranks(here, index, rank, hidden, adapters, packed):
    hbm = pl.BlockSpec(memory_space=pl.ANY)
    return pl.pallas_call(
        rank_kernel,
        grid_spec=pltpu.PrefetchScalarGridSpec(
            num_scalar_prefetch=3,
            grid=(1,),
            in_specs=[
                pl.BlockSpec((TOK, WIDTH), lambda i, here, index, rank: (0, 0)),
                pl.BlockSpec((1, RANK, WIDTH), lambda i, here, index, rank: (holder(here, index), 0, 0)),
                hbm,
            ],
            out_specs=hbm,
            scratch_shapes=[pltpu.VMEM((HALF, 2 * RANK), bf16), pltpu.SemaphoreType.DMA((HEADS,))],
        ),
        out_shape=jax.ShapeDtypeStruct(packed.shape, bf16),
        input_output_aliases={5: 0},
        compiler_params=params(32),
        cost_estimate=pl.CostEstimate(
            flops=2 * TOK * WIDTH * RANK, bytes_accessed=4 << 20, transcendentals=0
        ),
    )(here, index, rank, hidden, adapters, packed)


def image_kernel(here_ref, owner_ref, wk_ref, wv_ref, *refs):
    pieces, outs, kv = refs[:8], refs[8 : 8 + GROUPS], refs[8 + GROUPS]
    weights = jnp.concatenate([wk_ref[...], wv_ref[...]], axis=1)
    for p, piece in enumerate(pieces):
        half, shift = p // 4, p % 4
        rows = jnp.dot(piece[...], weights, preferred_element_type=f32).reshape(4, 4, 8, 2 * HD)
        for i in range(4):
            kv[half * 4 + i, shift * 32 : (shift + 1) * 32] = rows[:, i].reshape(32, 2 * HD)
    y, core = here_ref[0] // 2, here_ref[0] % 2
    for t in range(GROUPS):
        target = (y + t // 2) % 4 * 2 + (core + t % 2) % 2
        seen, held = jnp.int32(0), [jnp.int32(-1), jnp.int32(-1)]
        for i in range(8):
            hit = owner_ref[i] == target
            held = [jnp.where(hit & (seen == c), i, held[c]) for c in range(CAP)]
            seen = seen + hit.astype(jnp.int32)
        for c in range(CAP):
            got = kv[jnp.maximum(held[c], 0)]
            outs[t][c * IMG_TOK : (c + 1) * IMG_TOK] = jnp.where(held[c] >= 0, got, 0.0).astype(bf16)
        row = lax.broadcasted_iota(jnp.int32, (FLAG_ROWS, 2 * HD), 0)
        both = jnp.where(row == 0, held[0], held[1])
        outs[t][CAP * IMG_TOK :] = jnp.where(both >= 0, 1.0, 0.0).astype(bf16)


def place_images(here, owners, pieces, wk, wv):
    rows = CAP * IMG_TOK + FLAG_ROWS
    whole = pl.BlockSpec((ENC, HD), lambda i: (0, 0))
    return pl.pallas_call(
        image_kernel,
        grid=(1,),
        in_specs=[SMEM, SMEM, whole, whole] + [pl.BlockSpec((IMG_TOK, ENC), lambda i: (0, 0))] * 8,
        out_specs=[pl.BlockSpec((rows, 2 * HD), lambda i: (0, 0))] * GROUPS,
        out_shape=[jax.ShapeDtypeStruct((rows, 2 * HD), bf16)] * GROUPS,
        scratch_shapes=[pltpu.VMEM((8, IMG_TOK, 2 * HD), f32)],
        compiler_params=params(60),
        cost_estimate=pl.CostEstimate(
            flops=2 * 1024 * ENC * 2 * HD, bytes_accessed=5 << 20, transcendentals=0
        ),
    )(here, owners, wk, wv, *pieces)


def unpack_kernel(x_ref, o_ref):
    for h in range(HEADS):
        o_ref[0, :, h * HD : (h + 1) * HD] = x_ref[h]


def unpack_heads(per_head):
    rows = 128
    return pl.pallas_call(
        unpack_kernel,
        grid=(TOK // rows,),
        in_specs=[pl.BlockSpec((HEADS, rows, HD), lambda i: (0, i, 0))],
        out_specs=pl.BlockSpec((1, rows, HEADS * HD), lambda i: (0, i, 0)),
        out_shape=jax.ShapeDtypeStruct((1, TOK, HEADS * HD), bf16),
        compiler_params=pltpu.CompilerParams(vmem_limit_bytes=24 << 20),
        cost_estimate=pl.CostEstimate(flops=0, bytes_accessed=TOK * HEADS * HD * 4, transcendentals=0),
    )(per_head)


def transposed_scores(key, q):
    return lax.dot_general(key, q, NT, preferred_element_type=f32) * SCALE2


def weigh(val, p):
    return lax.dot_general(val, p.astype(bf16), TN, preferred_element_type=f32)


def by_eights(x):
    return x.reshape(x.shape[0] // 8, 8, x.shape[1])


def in_range(total):
    return (jnp.min(total) >= LEAST_TOTAL) & (jnp.max(total) <= LARGEST_TOTAL)


def self_key(kv_ref, chunk, c):
    blocks = chunk // HALF
    return kv_ref[c * blocks : (c + 1) * blocks, :HALF].reshape(chunk, HD)


def self_val(kv_ref, chunk, c):
    blocks = chunk // HALF
    return kv_ref[c * blocks : (c + 1) * blocks, HALF:].reshape(chunk, HD)


def none_yet(rows):
    return jnp.zeros((HD, rows), f32), jnp.zeros((8, rows), f32)


def self_part(kv_ref, q, chunk):
    acc, total = none_yet(q.shape[0])
    for c in range(HEADS * HALF // chunk):
        p = jnp.exp2(transposed_scores(self_key(kv_ref, chunk, c), q))
        total = total + by_eights(p).sum(0)
        acc = acc + weigh(self_val(kv_ref, chunk, c), p)
    return acc, jnp.sum(total, axis=0, keepdims=True)


def self_part_by_maximum(kv_ref, q, chunk):
    chunks, top = HEADS * HALF // chunk, jnp.full((8, q.shape[0]), -1e30, f32)
    for c in range(chunks):
        top = jnp.maximum(top, by_eights(transposed_scores(self_key(kv_ref, chunk, c), q)).max(0))
    top = jnp.max(top, axis=0, keepdims=True)
    acc, total = none_yet(q.shape[0])
    for c in range(chunks):
        p = jnp.exp2(transposed_scores(self_key(kv_ref, chunk, c), q) - top)
        total = total + by_eights(p).sum(0)
        acc = acc + weigh(self_val(kv_ref, chunk, c), p)
    return acc, jnp.sum(total, axis=0, keepdims=True), top


def slot_held(images, s):
    rows16 = images[s // CAP][CAP * IMG_TOK :, :HD].astype(f32)
    return rows16[s % CAP : s % CAP + 1, :1] > 0.5


def image_part(images, q, chunk):
    pairs, slots = chunk // (CAP * IMG_TOK), chunk // IMG_TOK

    def part(c, low):
        return jnp.concatenate(
            [images[c * pairs + i][: CAP * IMG_TOK, low : low + HD] for i in range(pairs)], axis=0
        )

    acc, total = none_yet(q.shape[0])
    for c in range(SLOTS // slots):
        p = jnp.exp2(transposed_scores(part(c, 0), q))
        per_slot = p.reshape(slots, IMG_TOK // 8, 8, q.shape[0]).sum(1)
        for s in range(slots):
            total = total + jnp.where(slot_held(images, c * slots + s), per_slot[s], 0.0)
        acc = acc + weigh(part(c, HD), p)
    return acc, jnp.sum(total, axis=0, keepdims=True)


def image_part_by_maximum(images, q):
    def slot_part(s, low):
        first = s % CAP * IMG_TOK
        return images[s // CAP][first : first + IMG_TOK, low : low + HD]

    def slot_scores(s):
        return jnp.where(slot_held(images, s), transposed_scores(slot_part(s, 0), q), -1e30)

    top = jnp.full((8, q.shape[0]), -1e30, f32)
    for s in range(SLOTS):
        top = jnp.maximum(top, by_eights(slot_scores(s)).max(0))
    top = jnp.max(top, axis=0, keepdims=True)
    acc, total = none_yet(q.shape[0])
    for s in range(SLOTS):
        p = jnp.exp2(slot_scores(s) - top)
        total = total + by_eights(p).sum(0)
        acc = acc + weigh(slot_part(s, HD), p)
    return acc, jnp.sum(total, axis=0, keepdims=True)


def first_kernel(
    here_ref, index_ref, rank_ref, q_ref, acts_ref, kv_ref, up_ref, *refs, per_step, chunk
):
    images, (q_s, acc_ref, sums_ref, img_ref, up_s) = refs[:GROUPS], refs[GROUPS:]

    @pl.when(pl.program_id(0) == 0)
    def _():
        up = up_ref[0]
        none = jnp.zeros_like(up)
        up_s[:, :HD] = jnp.concatenate([up, none], axis=0)
        up_s[:, HD:] = jnp.concatenate([none, up], axis=0)

    rank = jnp.full((1, 2 * HD), rank_ref[here_ref[0]].astype(f32))
    acts = acts_ref[...].reshape(per_step * HALF, 2 * RANK)
    update = adapter_alpha / rank * jnp.dot(acts, up_s[...], preferred_element_type=f32)
    parts = [update[:, half * HD : (half + 1) * HD].reshape(per_step, HALF, HD) for half in range(2)]
    q = (q_ref[...].astype(f32) + jnp.concatenate(parts, axis=1)).astype(bf16)
    q_s[...] = q
    q = q.reshape(per_step * TOK, HD)

    acc, total = self_part(kv_ref, q, chunk)
    img_acc, img_total = image_part(images, q, chunk)
    acc_ref[0] = acc
    sums_ref[0, :8] = jnp.broadcast_to(total, (8, total.shape[1]))
    sums_ref[0, 8:] = jnp.zeros((8, total.shape[1]), f32)
    img_ref[0] = img_acc / img_total

    @pl.when(jnp.logical_not(in_range(total)))
    def _():
        acc, total, top = self_part_by_maximum(kv_ref, q_s[...].reshape(per_step * TOK, HD), chunk)
        acc_ref[0] = acc
        sums_ref[0, :8] = jnp.broadcast_to(total, (8, total.shape[1]))
        sums_ref[0, 8:] = jnp.broadcast_to(top, (8, total.shape[1]))

    @pl.when(jnp.logical_not(in_range(img_total)))
    def _():
        acc, total = image_part_by_maximum(images, q_s[...].reshape(per_step * TOK, HD))
        img_ref[0] = acc / total


def second_kernel(q_ref, kv_ref, acc_ref, sums_ref, img_ref, o_ref, *, per_step, chunk):
    q = q_ref[...].reshape(per_step * TOK, HD)

    def emit(acc, total, top):
        total1, top1 = sums_ref[0, :1], sums_ref[0, 8:9]
        both = jnp.maximum(top, top1)
        scale, scale1 = jnp.exp2(top - both), jnp.exp2(top1 - both)
        own = (acc * scale + acc_ref[0] * scale1) / (total * scale + total1 * scale1)
        out = own + ip_scale * img_ref[0]
        o_ref[...] = out.T.astype(bf16).reshape(per_step, TOK, HD)

    acc, total = self_part(kv_ref, q, chunk)
    emit(acc, total, jnp.zeros_like(total))

    @pl.when(jnp.logical_not(in_range(total)))
    def _():
        emit(*self_part_by_maximum(kv_ref, q_ref[...].reshape(per_step * TOK, HD), chunk))


PER_STEP, CHUNK = 4, 1024
STEPS = HEADS // PER_STEP
HEAD_BLOCK = pl.BlockSpec((PER_STEP, TOK, HD), lambda i: (i, 0, 0))
KEYS_BLOCK = pl.BlockSpec((HEADS, TOK, HD), lambda i: (0, 0, 0))
WIDE_BLOCK = pl.BlockSpec((1, HD, PER_STEP * TOK), lambda i: (i, 0, 0))
SUMS_BLOCK = pl.BlockSpec((1, 16, PER_STEP * TOK), lambda i: (i, 0, 0))


def attention_cost(keys):
    pairs = HEADS * TOK * keys
    return pl.CostEstimate(flops=pairs * HD * 4, bytes_accessed=8 << 20, transcendentals=pairs)


def attend_first(here, index, rank, first, adapters, images):
    def block(shape, at):
        return pl.BlockSpec(shape, lambda i, here, index, rank: at(i, here, index))

    each = lambda i, here, index: (i, 0, 0)
    image = block((CAP * IMG_TOK + FLAG_ROWS, 2 * HD), lambda i, here, index: (0, 0))
    wide = jax.ShapeDtypeStruct((STEPS, HD, PER_STEP * TOK), f32)
    return pl.pallas_call(
        functools.partial(first_kernel, per_step=PER_STEP, chunk=CHUNK),
        grid_spec=pltpu.PrefetchScalarGridSpec(
            num_scalar_prefetch=3,
            grid=(STEPS,),
            in_specs=[
                block((PER_STEP, TOK, HD), lambda i, here, index: (i, 1, 0)),
                block((PER_STEP, 2 * RANK, HD), lambda i, here, index: (i, 2 * TOK // (2 * RANK), 0)),
                block((HEADS, TOK, HD), lambda i, here, index: (0, 0, 0)),
                block((1, RANK, HD), lambda i, here, index: (holder(here, index), 0, WIDTH // HD)),
            ]
            + [image] * GROUPS,
            out_specs=[
                block((PER_STEP, TOK, HD), each),
                block((1, HD, PER_STEP * TOK), each),
                block((1, 16, PER_STEP * TOK), each),
                block((1, HD, PER_STEP * TOK), each),
            ],
            scratch_shapes=[pltpu.VMEM((2 * RANK, 2 * HD), bf16)],
        ),
        out_shape=[
            jax.ShapeDtypeStruct((HEADS, TOK, HD), bf16),
            wide,
            jax.ShapeDtypeStruct((STEPS, 16, PER_STEP * TOK), f32),
            wide,
        ],
        compiler_params=params(60),
        cost_estimate=attention_cost(HEADS * HALF + SLOTS * IMG_TOK),
    )(here, index, rank, first, first, first, adapters, *images)


def attend_second(updated, second, acc, sums, image):
    return pl.pallas_call(
        functools.partial(second_kernel, per_step=PER_STEP, chunk=CHUNK),
        grid=(STEPS,),
        in_specs=[HEAD_BLOCK, KEYS_BLOCK, WIDE_BLOCK, SUMS_BLOCK, WIDE_BLOCK],
        out_specs=HEAD_BLOCK,
        out_shape=jax.ShapeDtypeStruct((HEADS, TOK, HD), bf16),
        compiler_params=params(60),
        cost_estimate=attention_cost(HEADS * HALF),
    )(updated, second, acc, sums, image)


def along_x(k):
    return [(z * 4 + x, z * 4 + (x + k) % 4) for z in range(4) for x in range(4)]


def along_z(k):
    return [(z * 4 + x, ((z + k) % 4) * 4 + x) for z in range(4) for x in range(4)]


def along_req(k, d):
    return [(y * 2 + c, (y + k) % 4 * 2 + (c + d) % 2) for y in range(4) for c in range(2)]


def exchange(x):
    return lax.all_to_all(x, "sp", split_axis=0, concat_axis=0, tiled=True)


def after(x, *others):
    return lax.optimization_barrier((x,) + others)[0]


def shards(
    hidden,
    latent_query_key_value,
    features,
    image_request,
    image_key_weight,
    image_value_weight,
    caller_lowfactor_index,
    request_rank,
    lowfactor_reducing_matrix,
    lowfactor_expanding_matrix,
):
    here = lax.axis_index("req").reshape(1)
    place = lax.axis_index("sp").reshape(1)
    index, rank = caller_lowfactor_index, request_rank
    planes = latent_query_key_value[0].transpose(1, 0, 2)

    own = jnp.concatenate(
        [
            lowfactor_reducing_matrix.transpose(0, 2, 1),
            lax.dynamic_slice_in_dim(lowfactor_expanding_matrix, place[0] * HD, HD, 2),
        ],
        axis=2,
    )
    other = lax.ppermute(own, "req", along_req(0, 1))

    half = features.shape[0] // 2
    lines = []
    for part, way in ((features[:half], along_x), (features[half:], along_z)):
        line = [part] + [lax.ppermute(part, "sp", way(k)) for k in (1, 2, 3)]
        lines.append(jnp.stack(line).reshape(IMG_TOK, ENC))
    pieces = []
    for line, way in zip(lines, (along_z, along_x)):
        pieces += [line] + [lax.ppermute(line, "sp", way(k)) for k in (1, 2, 3)]

    chosen = choose_adapters(here, index, own, other)
    adapters = lax.all_to_all(
        chosen,
        "req",
        split_axis=0,
        concat_axis=0,
        tiled=True,
        axis_index_groups=[[y * 2 + core for y in range(4)] for core in range(2)],
    )

    packed = add_ranks(here, index, rank, hidden[0], adapters, pack_first(planes))
    first = exchange(after(packed, *pieces))

    ways = [(k, d) for k in range(4) for d in range(2)]
    placed = place_images(here, image_request[:, 0], pieces, image_key_weight, image_value_weight)
    images = [placed[0]] + [
        lax.ppermute(p, "req", along_req(k, d)) for p, (k, d) in zip(placed[1:], ways[1:])
    ]

    second = exchange(after(pack_second(planes), first, *images))
    updated, acc, sums, image = attend_first(here, index, rank, first, adapters, images)
    per_heads = attend_second(updated, second, acc, sums, image)
    return unpack_heads(exchange(per_heads))


def solution(mesh):
    placed = (
        P("req", "sp", None),
        P("req", "sp", None, None),
        P("req", "sp", None),
        P("req", None),
        P(None, "sp"),
        P(None, "sp"),
        P(),
        P(),
        P("req", None, None),
        P("req", None, None),
    )
    return jax.shard_map(
        shards, mesh=mesh, in_specs=placed, out_specs=P("req", "sp", None), check_vma=False
    )
```

```python
import functools

import numpy as np

import jax
import jax.numpy as jnp
from jax import lax
from jax.experimental import pallas as pl
from jax.experimental.pallas import tpu as pltpu
from jax.sharding import PartitionSpec as P

HD = 128
CAP = 2
TOK = 256
HEADS = 16
GROUPS = 8
SLOTS = GROUPS * CAP
IMG_TOK = 128
ENC = 1152
RANK = 64
WIDTH = 3072
FLAG_ROWS = 16
HALF = TOK // 2
PACKED = 2 * TOK + 2 * RANK

adapter_alpha = 16.0
ip_scale = 1.0

SCALE2 = float(np.log2(np.e) / np.sqrt(HD))
LEAST_TOTAL, LARGEST_TOTAL = 2.0**-80, 2.0**96

bf16 = jnp.bfloat16
f32 = jnp.float32
NT = (((1,), (1,)), ((), ()))
TN = (((0,), (0,)), ((), ()))


SMEM = pl.BlockSpec(memory_space=pltpu.SMEM)


def params(mib):
    return pltpu.CompilerParams(vmem_limit_bytes=mib << 20)


def moving(nbytes):
    return pl.CostEstimate(flops=0, bytes_accessed=nbytes, transcendentals=0)


def pack_first_kernel(k_ref, v_ref, q_ref, o_ref):
    for h in range(HEADS):
        o_ref[h, :HALF] = k_ref[0, :, h * HD : (h + 1) * HD]
        o_ref[h, HALF:TOK] = v_ref[0, :, h * HD : (h + 1) * HD]
        o_ref[h, TOK:] = q_ref[0, :, h * HD : (h + 1) * HD]


def pack_second_kernel(k_ref, v_ref, o_ref):
    for h in range(HEADS):
        o_ref[h, :HALF] = k_ref[0, :, h * HD : (h + 1) * HD]
        o_ref[h, HALF:] = v_ref[0, :, h * HD : (h + 1) * HD]


def half_of(plane, part):
    return pl.BlockSpec((1, HALF, HEADS * HD), lambda i: (plane, part, 0))


def pack_first(planes):
    return pl.pallas_call(
        pack_first_kernel,
        grid=(1,),
        in_specs=[half_of(1, 0), half_of(2, 0), pl.BlockSpec((1, TOK, HEADS * HD), lambda i: (0, 0, 0))],
        out_specs=pl.BlockSpec((HEADS, 2 * TOK, HD), lambda i: (0, 0, 0)),
        out_shape=jax.ShapeDtypeStruct((HEADS, PACKED, HD), bf16),
        compiler_params=params(24),
        cost_estimate=moving(4 << 20),
    )(planes, planes, planes)


def pack_second(planes):
    return pl.pallas_call(
        pack_second_kernel,
        grid=(1,),
        in_specs=[half_of(1, 1), half_of(2, 1)],
        out_specs=pl.BlockSpec((HEADS, TOK, HD), lambda i: (0, 0, 0)),
        out_shape=jax.ShapeDtypeStruct((HEADS, TOK, HD), bf16),
        compiler_params=params(24),
        cost_estimate=moving(2 << 20),
    )(planes, planes)


def choose_kernel(here_ref, index_ref, own_ref, other_ref, o_ref, sems):
    core = here_ref[0] % 2
    for y in range(4):
        local = index_ref[y * 2 + core] % 4

        @pl.when(local // 2 == core)
        def _():
            pltpu.make_async_copy(own_ref.at[local % 2], o_ref.at[y], sems.at[y]).start()

        @pl.when(local // 2 != core)
        def _():
            pltpu.make_async_copy(other_ref.at[local % 2], o_ref.at[y], sems.at[y]).start()

    for y in range(4):
        pltpu.make_async_copy(own_ref.at[0], o_ref.at[y], sems.at[y]).wait()


def choose_adapters(here, index, own, other):
    hbm = pl.BlockSpec(memory_space=pl.ANY)
    return pl.pallas_call(
        choose_kernel,
        in_specs=[SMEM, SMEM, hbm, hbm],
        out_specs=hbm,
        scratch_shapes=[pltpu.SemaphoreType.DMA((4,))],
        out_shape=jax.ShapeDtypeStruct((4,) + own.shape[1:], bf16),
        compiler_params=params(24),
        cost_estimate=moving(own.size * 8),
    )(here, index, own, other)


def holder(here, index):
    return index[here[0]] // 4


def rank_kernel(here_ref, index_ref, rank_ref, hidden_ref, a_ref, _, o_ref, acts_ref, sems):
    acts = lax.dot_general(hidden_ref[...], a_ref[0], NT, preferred_element_type=f32)
    kept = lax.broadcasted_iota(jnp.int32, acts.shape, 1) < rank_ref[here_ref[0]]
    acts = jnp.where(kept, acts, 0.0)
    acts_ref[...] = jnp.concatenate([acts[:HALF], acts[HALF:]], axis=1).astype(bf16)
    copies = [
        pltpu.make_async_copy(acts_ref, o_ref.at[h, pl.ds(2 * TOK, 2 * RANK)], sems.at[h])
        for h in range(HEADS)
    ]
    for copy in copies:
        copy.start()
    for copy in copies:
        copy.wait()


def add_ranks(here, index, rank, hidden, adapters, packed):
    hbm = pl.BlockSpec(memory_space=pl.ANY)
    return pl.pallas_call(
        rank_kernel,
        grid_spec=pltpu.PrefetchScalarGridSpec(
            num_scalar_prefetch=3,
            grid=(1,),
            in_specs=[
                pl.BlockSpec((TOK, WIDTH), lambda i, here, index, rank: (0, 0)),
                pl.BlockSpec((1, RANK, WIDTH), lambda i, here, index, rank: (holder(here, index), 0, 0)),
                hbm,
            ],
            out_specs=hbm,
            scratch_shapes=[pltpu.VMEM((HALF, 2 * RANK), bf16), pltpu.SemaphoreType.DMA((HEADS,))],
        ),
        out_shape=jax.ShapeDtypeStruct(packed.shape, bf16),
        input_output_aliases={5: 0},
        compiler_params=params(32),
        cost_estimate=pl.CostEstimate(
            flops=2 * TOK * WIDTH * RANK, bytes_accessed=4 << 20, transcendentals=0
        ),
    )(here, index, rank, hidden, adapters, packed)


def image_kernel(here_ref, owner_ref, wk_ref, wv_ref, *refs):
    pieces, outs, kv = refs[:8], refs[8 : 8 + GROUPS], refs[8 + GROUPS]
    weights = jnp.concatenate([wk_ref[...], wv_ref[...]], axis=1)
    for p, piece in enumerate(pieces):
        half, shift = p // 4, p % 4
        rows = jnp.dot(piece[...], weights, preferred_element_type=f32).reshape(4, 4, 8, 2 * HD)
        for i in range(4):
            kv[half * 4 + i, shift * 32 : (shift + 1) * 32] = rows[:, i].reshape(32, 2 * HD)
    y, core = here_ref[0] // 2, here_ref[0] % 2
    for t in range(GROUPS):
        target = (y + t // 2) % 4 * 2 + (core + t % 2) % 2
        seen, held = jnp.int32(0), [jnp.int32(-1), jnp.int32(-1)]
        for i in range(8):
            hit = owner_ref[i] == target
            held = [jnp.where(hit & (seen == c), i, held[c]) for c in range(CAP)]
            seen = seen + hit.astype(jnp.int32)
        for c in range(CAP):
            got = kv[jnp.maximum(held[c], 0)]
            outs[t][c * IMG_TOK : (c + 1) * IMG_TOK] = jnp.where(held[c] >= 0, got, 0.0).astype(bf16)
        row = lax.broadcasted_iota(jnp.int32, (FLAG_ROWS, 2 * HD), 0)
        both = jnp.where(row == 0, held[0], held[1])
        outs[t][CAP * IMG_TOK :] = jnp.where(both >= 0, 1.0, 0.0).astype(bf16)


def place_images(here, owners, pieces, wk, wv):
    rows = CAP * IMG_TOK + FLAG_ROWS
    whole = pl.BlockSpec((ENC, HD), lambda i: (0, 0))
    return pl.pallas_call(
        image_kernel,
        grid=(1,),
        in_specs=[SMEM, SMEM, whole, whole] + [pl.BlockSpec((IMG_TOK, ENC), lambda i: (0, 0))] * 8,
        out_specs=[pl.BlockSpec((rows, 2 * HD), lambda i: (0, 0))] * GROUPS,
        out_shape=[jax.ShapeDtypeStruct((rows, 2 * HD), bf16)] * GROUPS,
        scratch_shapes=[pltpu.VMEM((8, IMG_TOK, 2 * HD), f32)],
        compiler_params=params(60),
        cost_estimate=pl.CostEstimate(
            flops=2 * 1024 * ENC * 2 * HD, bytes_accessed=5 << 20, transcendentals=0
        ),
    )(here, owners, wk, wv, *pieces)


def unpack_kernel(x_ref, o_ref):
    for h in range(HEADS):
        o_ref[0, :, h * HD : (h + 1) * HD] = x_ref[h]


def unpack_heads(per_head):
    rows = 128
    return pl.pallas_call(
        unpack_kernel,
        grid=(TOK // rows,),
        in_specs=[pl.BlockSpec((HEADS, rows, HD), lambda i: (0, i, 0))],
        out_specs=pl.BlockSpec((1, rows, HEADS * HD), lambda i: (0, i, 0)),
        out_shape=jax.ShapeDtypeStruct((1, TOK, HEADS * HD), bf16),
        compiler_params=pltpu.CompilerParams(vmem_limit_bytes=24 << 20),
        cost_estimate=pl.CostEstimate(flops=0, bytes_accessed=TOK * HEADS * HD * 4, transcendentals=0),
    )(per_head)


def transposed_scores(key, q):
    return lax.dot_general(key, q, NT, preferred_element_type=f32) * SCALE2


def weigh(val, p):
    return lax.dot_general(val, p.astype(bf16), TN, preferred_element_type=f32)


def by_eights(x):
    return x.reshape(x.shape[0] // 8, 8, x.shape[1])


def in_range(total):
    return (jnp.min(total) >= LEAST_TOTAL) & (jnp.max(total) <= LARGEST_TOTAL)


def self_key(kv_ref, chunk, c):
    blocks = chunk // HALF
    return kv_ref[c * blocks : (c + 1) * blocks, :HALF].reshape(chunk, HD)


def self_val(kv_ref, chunk, c):
    blocks = chunk // HALF
    return kv_ref[c * blocks : (c + 1) * blocks, HALF:].reshape(chunk, HD)


def none_yet(rows):
    return jnp.zeros((HD, rows), f32), jnp.zeros((8, rows), f32)


def self_part(kv_ref, q, chunk):
    acc, total = none_yet(q.shape[0])
    for c in range(HEADS * HALF // chunk):
        p = jnp.exp2(transposed_scores(self_key(kv_ref, chunk, c), q))
        total = total + by_eights(p).sum(0)
        acc = acc + weigh(self_val(kv_ref, chunk, c), p)
    return acc, jnp.sum(total, axis=0, keepdims=True)


def self_part_by_maximum(kv_ref, q, chunk):
    chunks, top = HEADS * HALF // chunk, jnp.full((8, q.shape[0]), -1e30, f32)
    for c in range(chunks):
        top = jnp.maximum(top, by_eights(transposed_scores(self_key(kv_ref, chunk, c), q)).max(0))
    top = jnp.max(top, axis=0, keepdims=True)
    acc, total = none_yet(q.shape[0])
    for c in range(chunks):
        p = jnp.exp2(transposed_scores(self_key(kv_ref, chunk, c), q) - top)
        total = total + by_eights(p).sum(0)
        acc = acc + weigh(self_val(kv_ref, chunk, c), p)
    return acc, jnp.sum(total, axis=0, keepdims=True), top


def slot_held(images, s):
    rows16 = images[s // CAP][CAP * IMG_TOK :, :HD].astype(f32)
    return rows16[s % CAP : s % CAP + 1, :1] > 0.5


def image_part(images, q, chunk):
    pairs, slots = chunk // (CAP * IMG_TOK), chunk // IMG_TOK

    def part(c, low):
        return jnp.concatenate(
            [images[c * pairs + i][: CAP * IMG_TOK, low : low + HD] for i in range(pairs)], axis=0
        )

    acc, total = none_yet(q.shape[0])
    for c in range(SLOTS // slots):
        p = jnp.exp2(transposed_scores(part(c, 0), q))
        per_slot = p.reshape(slots, IMG_TOK // 8, 8, q.shape[0]).sum(1)
        for s in range(slots):
            total = total + jnp.where(slot_held(images, c * slots + s), per_slot[s], 0.0)
        acc = acc + weigh(part(c, HD), p)
    return acc, jnp.sum(total, axis=0, keepdims=True)


def image_part_by_maximum(images, q):
    def slot_part(s, low):
        first = s % CAP * IMG_TOK
        return images[s // CAP][first : first + IMG_TOK, low : low + HD]

    def slot_scores(s):
        return jnp.where(slot_held(images, s), transposed_scores(slot_part(s, 0), q), -1e30)

    top = jnp.full((8, q.shape[0]), -1e30, f32)
    for s in range(SLOTS):
        top = jnp.maximum(top, by_eights(slot_scores(s)).max(0))
    top = jnp.max(top, axis=0, keepdims=True)
    acc, total = none_yet(q.shape[0])
    for s in range(SLOTS):
        p = jnp.exp2(slot_scores(s) - top)
        total = total + by_eights(p).sum(0)
        acc = acc + weigh(slot_part(s, HD), p)
    return acc, jnp.sum(total, axis=0, keepdims=True)


def first_kernel(
    here_ref, index_ref, rank_ref, q_ref, acts_ref, kv_ref, up_ref, *refs, per_step, chunk
):
    images, (q_s, acc_ref, sums_ref, img_ref, up_s) = refs[:GROUPS], refs[GROUPS:]

    @pl.when(pl.program_id(0) == 0)
    def _():
        up = up_ref[0]
        none = jnp.zeros_like(up)
        up_s[:, :HD] = jnp.concatenate([up, none], axis=0)
        up_s[:, HD:] = jnp.concatenate([none, up], axis=0)

    rank = jnp.full((1, 2 * HD), rank_ref[here_ref[0]].astype(f32))
    acts = acts_ref[...].reshape(per_step * HALF, 2 * RANK)
    update = adapter_alpha / rank * jnp.dot(acts, up_s[...], preferred_element_type=f32)
    parts = [update[:, half * HD : (half + 1) * HD].reshape(per_step, HALF, HD) for half in range(2)]
    q = (q_ref[...].astype(f32) + jnp.concatenate(parts, axis=1)).astype(bf16)
    q_s[...] = q
    q = q.reshape(per_step * TOK, HD)

    acc, total = self_part(kv_ref, q, chunk)
    img_acc, img_total = image_part(images, q, chunk)
    acc_ref[0] = acc
    sums_ref[0, :8] = jnp.broadcast_to(total, (8, total.shape[1]))
    sums_ref[0, 8:] = jnp.zeros((8, total.shape[1]), f32)
    img_ref[0] = img_acc / img_total

    @pl.when(jnp.logical_not(in_range(total)))
    def _():
        acc, total, top = self_part_by_maximum(kv_ref, q_s[...].reshape(per_step * TOK, HD), chunk)
        acc_ref[0] = acc
        sums_ref[0, :8] = jnp.broadcast_to(total, (8, total.shape[1]))
        sums_ref[0, 8:] = jnp.broadcast_to(top, (8, total.shape[1]))

    @pl.when(jnp.logical_not(in_range(img_total)))
    def _():
        acc, total = image_part_by_maximum(images, q_s[...].reshape(per_step * TOK, HD))
        img_ref[0] = acc / total


def second_kernel(q_ref, kv_ref, acc_ref, sums_ref, img_ref, o_ref, *, per_step, chunk):
    q = q_ref[...].reshape(per_step * TOK, HD)

    def emit(acc, total, top):
        total1, top1 = sums_ref[0, :1], sums_ref[0, 8:9]
        both = jnp.maximum(top, top1)
        scale, scale1 = jnp.exp2(top - both), jnp.exp2(top1 - both)
        own = (acc * scale + acc_ref[0] * scale1) / (total * scale + total1 * scale1)
        out = own + ip_scale * img_ref[0]
        o_ref[...] = out.astype(bf16).T.reshape(per_step, TOK, HD)

    acc, total = self_part(kv_ref, q, chunk)
    emit(acc, total, jnp.zeros_like(total))

    @pl.when(jnp.logical_not(in_range(total)))
    def _():
        emit(*self_part_by_maximum(kv_ref, q_ref[...].reshape(per_step * TOK, HD), chunk))


PER_STEP, CHUNK = 4, 1024
STEPS = HEADS // PER_STEP
HEAD_BLOCK = pl.BlockSpec((PER_STEP, TOK, HD), lambda i: (i, 0, 0))
KEYS_BLOCK = pl.BlockSpec((HEADS, TOK, HD), lambda i: (0, 0, 0))
WIDE_BLOCK = pl.BlockSpec((1, HD, PER_STEP * TOK), lambda i: (i, 0, 0))
SUMS_BLOCK = pl.BlockSpec((1, 16, PER_STEP * TOK), lambda i: (i, 0, 0))


def attention_cost(keys):
    pairs = HEADS * TOK * keys
    return pl.CostEstimate(flops=pairs * HD * 4, bytes_accessed=8 << 20, transcendentals=pairs)


def attend_first(here, index, rank, first, adapters, images):
    def block(shape, at):
        return pl.BlockSpec(shape, lambda i, here, index, rank: at(i, here, index))

    each = lambda i, here, index: (i, 0, 0)
    image = block((CAP * IMG_TOK + FLAG_ROWS, 2 * HD), lambda i, here, index: (0, 0))
    wide = jax.ShapeDtypeStruct((STEPS, HD, PER_STEP * TOK), f32)
    return pl.pallas_call(
        functools.partial(first_kernel, per_step=PER_STEP, chunk=CHUNK),
        grid_spec=pltpu.PrefetchScalarGridSpec(
            num_scalar_prefetch=3,
            grid=(STEPS,),
            in_specs=[
                block((PER_STEP, TOK, HD), lambda i, here, index: (i, 1, 0)),
                block((PER_STEP, 2 * RANK, HD), lambda i, here, index: (i, 2 * TOK // (2 * RANK), 0)),
                block((HEADS, TOK, HD), lambda i, here, index: (0, 0, 0)),
                block((1, RANK, HD), lambda i, here, index: (holder(here, index), 0, WIDTH // HD)),
            ]
            + [image] * GROUPS,
            out_specs=[
                block((PER_STEP, TOK, HD), each),
                block((1, HD, PER_STEP * TOK), each),
                block((1, 16, PER_STEP * TOK), each),
                block((1, HD, PER_STEP * TOK), each),
            ],
            scratch_shapes=[pltpu.VMEM((2 * RANK, 2 * HD), bf16)],
        ),
        out_shape=[
            jax.ShapeDtypeStruct((HEADS, TOK, HD), bf16),
            wide,
            jax.ShapeDtypeStruct((STEPS, 16, PER_STEP * TOK), f32),
            wide,
        ],
        compiler_params=params(60),
        cost_estimate=attention_cost(HEADS * HALF + SLOTS * IMG_TOK),
    )(here, index, rank, first, first, first, adapters, *images)


def attend_second(updated, second, acc, sums, image):
    return pl.pallas_call(
        functools.partial(second_kernel, per_step=PER_STEP, chunk=CHUNK),
        grid=(STEPS,),
        in_specs=[HEAD_BLOCK, KEYS_BLOCK, WIDE_BLOCK, SUMS_BLOCK, WIDE_BLOCK],
        out_specs=HEAD_BLOCK,
        out_shape=jax.ShapeDtypeStruct((HEADS, TOK, HD), bf16),
        compiler_params=params(60),
        cost_estimate=attention_cost(HEADS * HALF),
    )(updated, second, acc, sums, image)


def along_x(k):
    return [(z * 4 + x, z * 4 + (x + k) % 4) for z in range(4) for x in range(4)]


def along_z(k):
    return [(z * 4 + x, ((z + k) % 4) * 4 + x) for z in range(4) for x in range(4)]


def along_req(k, d):
    return [(y * 2 + c, (y + k) % 4 * 2 + (c + d) % 2) for y in range(4) for c in range(2)]


def exchange(x):
    return lax.all_to_all(x, "sp", split_axis=0, concat_axis=0, tiled=True)


def after(x, *others):
    return lax.optimization_barrier((x,) + others)[0]


def shards(
    hidden,
    latent_query_key_value,
    features,
    image_request,
    image_key_weight,
    image_value_weight,
    caller_lowfactor_index,
    request_rank,
    lowfactor_reducing_matrix,
    lowfactor_expanding_matrix,
):
    here = lax.axis_index("req").reshape(1)
    place = lax.axis_index("sp").reshape(1)
    index, rank = caller_lowfactor_index, request_rank
    planes = latent_query_key_value[0].transpose(1, 0, 2)

    own = jnp.concatenate(
        [
            lowfactor_reducing_matrix.transpose(0, 2, 1),
            lax.dynamic_slice_in_dim(lowfactor_expanding_matrix, place[0] * HD, HD, 2),
        ],
        axis=2,
    )
    other = lax.ppermute(own, "req", along_req(0, 1))

    half = features.shape[0] // 2
    lines = []
    for part, way in ((features[:half], along_x), (features[half:], along_z)):
        line = [part] + [lax.ppermute(part, "sp", way(k)) for k in (1, 2, 3)]
        lines.append(jnp.stack(line).reshape(IMG_TOK, ENC))
    pieces = []
    for line, way in zip(lines, (along_z, along_x)):
        pieces += [line] + [lax.ppermute(line, "sp", way(k)) for k in (1, 2, 3)]

    chosen = choose_adapters(here, index, own, other)
    adapters = lax.all_to_all(
        chosen,
        "req",
        split_axis=0,
        concat_axis=0,
        tiled=True,
        axis_index_groups=[[y * 2 + core for y in range(4)] for core in range(2)],
    )

    packed = add_ranks(here, index, rank, hidden[0], adapters, pack_first(planes))
    first = exchange(after(packed, *pieces))

    ways = [(k, d) for k in range(4) for d in range(2)]
    placed = place_images(here, image_request[:, 0], pieces, image_key_weight, image_value_weight)
    images = [placed[0]] + [
        lax.ppermute(p, "req", along_req(k, d)) for p, (k, d) in zip(placed[1:], ways[1:])
    ]

    second = exchange(after(pack_second(planes), first, *images))
    updated, acc, sums, image = attend_first(here, index, rank, first, adapters, images)
    per_heads = attend_second(updated, second, acc, sums, image)
    return unpack_heads(exchange(per_heads))


def solution(mesh):
    placed = (
        P("req", "sp", None),
        P("req", "sp", None, None),
        P("req", "sp", None),
        P("req", None),
        P(None, "sp"),
        P(None, "sp"),
        P(),
        P(),
        P("req", None, None),
        P("req", None, None),
    )
    return jax.shard_map(
        shards, mesh=mesh, in_specs=placed, out_specs=P("req", "sp", None), check_vma=False
    )
```

```python
import functools

import numpy as np

import jax
import jax.numpy as jnp
from jax import lax
from jax.experimental import pallas as pl
from jax.experimental.pallas import tpu as pltpu
from jax.sharding import PartitionSpec as P

HD = 128
CAP = 2
TOK = 256
HEADS = 16
GROUPS = 8
SLOTS = GROUPS * CAP
IMG_TOK = 128
ENC = 1152
RANK = 64
WIDTH = 3072
FLAG_ROWS = 16
HALF = TOK // 2
PACKED = 2 * TOK + 2 * RANK

adapter_alpha = 16.0
ip_scale = 1.0

SCALE2 = float(np.log2(np.e) / np.sqrt(HD))
LEAST_TOTAL, LARGEST_TOTAL = 2.0**-80, 2.0**96

bf16 = jnp.bfloat16
f32 = jnp.float32
NT = (((1,), (1,)), ((), ()))
TN = (((0,), (0,)), ((), ()))


SMEM = pl.BlockSpec(memory_space=pltpu.SMEM)


def params(mib):
    return pltpu.CompilerParams(vmem_limit_bytes=mib << 20)


def moving(nbytes):
    return pl.CostEstimate(flops=0, bytes_accessed=nbytes, transcendentals=0)


def pack_first_kernel(k_ref, v_ref, q_ref, o_ref):
    for h in range(HEADS):
        o_ref[h, :HALF] = k_ref[0, :, h * HD : (h + 1) * HD]
        o_ref[h, HALF:TOK] = v_ref[0, :, h * HD : (h + 1) * HD]
        o_ref[h, TOK:] = q_ref[0, :, h * HD : (h + 1) * HD]


def pack_second_kernel(k_ref, v_ref, o_ref):
    for h in range(HEADS):
        o_ref[h, :HALF] = k_ref[0, :, h * HD : (h + 1) * HD]
        o_ref[h, HALF:] = v_ref[0, :, h * HD : (h + 1) * HD]


def half_of(plane, part):
    return pl.BlockSpec((1, HALF, HEADS * HD), lambda i: (plane, part, 0))


def pack_first(planes):
    return pl.pallas_call(
        pack_first_kernel,
        grid=(1,),
        in_specs=[half_of(1, 0), half_of(2, 0), pl.BlockSpec((1, TOK, HEADS * HD), lambda i: (0, 0, 0))],
        out_specs=pl.BlockSpec((HEADS, 2 * TOK, HD), lambda i: (0, 0, 0)),
        out_shape=jax.ShapeDtypeStruct((HEADS, PACKED, HD), bf16),
        compiler_params=params(24),
        cost_estimate=moving(4 << 20),
    )(planes, planes, planes)


def pack_second(planes):
    return pl.pallas_call(
        pack_second_kernel,
        grid=(1,),
        in_specs=[half_of(1, 1), half_of(2, 1)],
        out_specs=pl.BlockSpec((HEADS, TOK, HD), lambda i: (0, 0, 0)),
        out_shape=jax.ShapeDtypeStruct((HEADS, TOK, HD), bf16),
        compiler_params=params(24),
        cost_estimate=moving(2 << 20),
    )(planes, planes)


def choose_kernel(here_ref, index_ref, own_ref, other_ref, o_ref, sems):
    core = here_ref[0] % 2
    for y in range(4):
        local = index_ref[y * 2 + core] % 4

        @pl.when(local // 2 == core)
        def _():
            pltpu.make_async_copy(own_ref.at[local % 2], o_ref.at[y], sems.at[y]).start()

        @pl.when(local // 2 != core)
        def _():
            pltpu.make_async_copy(other_ref.at[local % 2], o_ref.at[y], sems.at[y]).start()

    for y in range(4):
        pltpu.make_async_copy(own_ref.at[0], o_ref.at[y], sems.at[y]).wait()


def choose_adapters(here, index, own, other):
    hbm = pl.BlockSpec(memory_space=pl.ANY)
    return pl.pallas_call(
        choose_kernel,
        in_specs=[SMEM, SMEM, hbm, hbm],
        out_specs=hbm,
        scratch_shapes=[pltpu.SemaphoreType.DMA((4,))],
        out_shape=jax.ShapeDtypeStruct((4,) + own.shape[1:], bf16),
        compiler_params=params(24),
        cost_estimate=moving(own.size * 8),
    )(here, index, own, other)


def holder(here, index):
    return index[here[0]] // 4


def rank_kernel(here_ref, index_ref, rank_ref, hidden_ref, a_ref, _, o_ref, acts_ref, sems):
    acts = lax.dot_general(hidden_ref[...], a_ref[0], NT, preferred_element_type=f32)
    kept = lax.broadcasted_iota(jnp.int32, acts.shape, 1) < rank_ref[here_ref[0]]
    acts = jnp.where(kept, acts, 0.0)
    acts_ref[...] = jnp.concatenate([acts[:HALF], acts[HALF:]], axis=1).astype(bf16)
    copies = [
        pltpu.make_async_copy(acts_ref, o_ref.at[h, pl.ds(2 * TOK, 2 * RANK)], sems.at[h])
        for h in range(HEADS)
    ]
    for copy in copies:
        copy.start()
    for copy in copies:
        copy.wait()


def add_ranks(here, index, rank, hidden, adapters, packed):
    hbm = pl.BlockSpec(memory_space=pl.ANY)
    return pl.pallas_call(
        rank_kernel,
        grid_spec=pltpu.PrefetchScalarGridSpec(
            num_scalar_prefetch=3,
            grid=(1,),
            in_specs=[
                pl.BlockSpec((TOK, WIDTH), lambda i, here, index, rank: (0, 0)),
                pl.BlockSpec((1, RANK, WIDTH), lambda i, here, index, rank: (holder(here, index), 0, 0)),
                hbm,
            ],
            out_specs=hbm,
            scratch_shapes=[pltpu.VMEM((HALF, 2 * RANK), bf16), pltpu.SemaphoreType.DMA((HEADS,))],
        ),
        out_shape=jax.ShapeDtypeStruct(packed.shape, bf16),
        input_output_aliases={5: 0},
        compiler_params=params(32),
        cost_estimate=pl.CostEstimate(
            flops=2 * TOK * WIDTH * RANK, bytes_accessed=4 << 20, transcendentals=0
        ),
    )(here, index, rank, hidden, adapters, packed)


def image_kernel(here_ref, owner_ref, wk_ref, wv_ref, *refs):
    pieces, outs, kv = refs[:8], refs[8 : 8 + GROUPS], refs[8 + GROUPS]
    weights = jnp.concatenate([wk_ref[...], wv_ref[...]], axis=1)
    for p, piece in enumerate(pieces):
        half, shift = p // 4, p % 4
        rows = jnp.dot(piece[...], weights, preferred_element_type=f32).reshape(4, 4, 8, 2 * HD)
        for i in range(4):
            kv[half * 4 + i, shift * 32 : (shift + 1) * 32] = rows[:, i].reshape(32, 2 * HD)
    y, core = here_ref[0] // 2, here_ref[0] % 2
    for t in range(GROUPS):
        target = (y + t // 2) % 4 * 2 + (core + t % 2) % 2
        seen, held = jnp.int32(0), [jnp.int32(-1), jnp.int32(-1)]
        for i in range(8):
            hit = owner_ref[i] == target
            held = [jnp.where(hit & (seen == c), i, held[c]) for c in range(CAP)]
            seen = seen + hit.astype(jnp.int32)
        for c in range(CAP):
            got = kv[jnp.maximum(held[c], 0)]
            outs[t][c * IMG_TOK : (c + 1) * IMG_TOK] = jnp.where(held[c] >= 0, got, 0.0).astype(bf16)
        row = lax.broadcasted_iota(jnp.int32, (FLAG_ROWS, 2 * HD), 0)
        both = jnp.where(row == 0, held[0], held[1])
        outs[t][CAP * IMG_TOK :] = jnp.where(both >= 0, 1.0, 0.0).astype(bf16)


def place_images(here, owners, pieces, wk, wv):
    rows = CAP * IMG_TOK + FLAG_ROWS
    whole = pl.BlockSpec((ENC, HD), lambda i: (0, 0))
    return pl.pallas_call(
        image_kernel,
        grid=(1,),
        in_specs=[SMEM, SMEM, whole, whole] + [pl.BlockSpec((IMG_TOK, ENC), lambda i: (0, 0))] * 8,
        out_specs=[pl.BlockSpec((rows, 2 * HD), lambda i: (0, 0))] * GROUPS,
        out_shape=[jax.ShapeDtypeStruct((rows, 2 * HD), bf16)] * GROUPS,
        scratch_shapes=[pltpu.VMEM((8, IMG_TOK, 2 * HD), f32)],
        compiler_params=params(60),
        cost_estimate=pl.CostEstimate(
            flops=2 * 1024 * ENC * 2 * HD, bytes_accessed=5 << 20, transcendentals=0
        ),
    )(here, owners, wk, wv, *pieces)


def unpack_kernel(x_ref, o_ref):
    for h in range(HEADS):
        o_ref[0, :, h * HD : (h + 1) * HD] = x_ref[h]


def unpack_heads(per_head):
    rows = 128
    return pl.pallas_call(
        unpack_kernel,
        grid=(TOK // rows,),
        in_specs=[pl.BlockSpec((HEADS, rows, HD), lambda i: (0, i, 0))],
        out_specs=pl.BlockSpec((1, rows, HEADS * HD), lambda i: (0, i, 0)),
        out_shape=jax.ShapeDtypeStruct((1, TOK, HEADS * HD), bf16),
        compiler_params=pltpu.CompilerParams(vmem_limit_bytes=24 << 20),
        cost_estimate=pl.CostEstimate(flops=0, bytes_accessed=TOK * HEADS * HD * 4, transcendentals=0),
    )(per_head)


def transposed_scores(key, q):
    return lax.dot_general(key, q, NT, preferred_element_type=f32) * SCALE2


def weigh(val, p):
    return lax.dot_general(val, p.astype(bf16), TN, preferred_element_type=f32)


def by_eights(x):
    return x.reshape(x.shape[0] // 8, 8, x.shape[1])


def in_range(total):
    return (jnp.min(total) >= LEAST_TOTAL) & (jnp.max(total) <= LARGEST_TOTAL)


def self_key(kv_ref, chunk, c):
    blocks = chunk // HALF
    return kv_ref[c * blocks : (c + 1) * blocks, :HALF].reshape(chunk, HD)


def self_val(kv_ref, chunk, c):
    blocks = chunk // HALF
    return kv_ref[c * blocks : (c + 1) * blocks, HALF:].reshape(chunk, HD)


def none_yet(rows):
    return jnp.zeros((HD, rows), f32), jnp.zeros((8, rows), f32)


def self_part(kv_ref, q, chunk):
    acc, total = none_yet(q.shape[0])
    for c in range(HEADS * HALF // chunk):
        p = jnp.exp2(transposed_scores(self_key(kv_ref, chunk, c), q))
        total = total + by_eights(p).sum(0)
        acc = acc + weigh(self_val(kv_ref, chunk, c), p)
    return acc, jnp.sum(total, axis=0, keepdims=True)


def self_part_by_maximum(kv_ref, q, chunk):
    chunks, top = HEADS * HALF // chunk, jnp.full((8, q.shape[0]), -1e30, f32)
    for c in range(chunks):
        top = jnp.maximum(top, by_eights(transposed_scores(self_key(kv_ref, chunk, c), q)).max(0))
    top = jnp.max(top, axis=0, keepdims=True)
    acc, total = none_yet(q.shape[0])
    for c in range(chunks):
        p = jnp.exp2(transposed_scores(self_key(kv_ref, chunk, c), q) - top)
        total = total + by_eights(p).sum(0)
        acc = acc + weigh(self_val(kv_ref, chunk, c), p)
    return acc, jnp.sum(total, axis=0, keepdims=True), top


def slot_held(images, s):
    rows16 = images[s // CAP][CAP * IMG_TOK :, :HD].astype(f32)
    return rows16[s % CAP : s % CAP + 1, :1] > 0.5


def image_part(images, q, chunk):
    pairs, slots = chunk // (CAP * IMG_TOK), chunk // IMG_TOK

    def part(c, low):
        return jnp.concatenate(
            [images[c * pairs + i][: CAP * IMG_TOK, low : low + HD] for i in range(pairs)], axis=0
        )

    acc, total = none_yet(q.shape[0])
    for c in range(SLOTS // slots):
        p = jnp.exp2(transposed_scores(part(c, 0), q))
        per_slot = p.reshape(slots, IMG_TOK // 8, 8, q.shape[0]).sum(1)
        for s in range(slots):
            total = total + jnp.where(slot_held(images, c * slots + s), per_slot[s], 0.0)
        acc = acc + weigh(part(c, HD), p)
    return acc, jnp.sum(total, axis=0, keepdims=True)


def image_part_by_maximum(images, q):
    def slot_part(s, low):
        first = s % CAP * IMG_TOK
        return images[s // CAP][first : first + IMG_TOK, low : low + HD]

    def slot_scores(s):
        return jnp.where(slot_held(images, s), transposed_scores(slot_part(s, 0), q), -1e30)

    top = jnp.full((8, q.shape[0]), -1e30, f32)
    for s in range(SLOTS):
        top = jnp.maximum(top, by_eights(slot_scores(s)).max(0))
    top = jnp.max(top, axis=0, keepdims=True)
    acc, total = none_yet(q.shape[0])
    for s in range(SLOTS):
        p = jnp.exp2(slot_scores(s) - top)
        total = total + by_eights(p).sum(0)
        acc = acc + weigh(slot_part(s, HD), p)
    return acc, jnp.sum(total, axis=0, keepdims=True)


def first_kernel(
    here_ref, index_ref, rank_ref, q_ref, acts_ref, kv_ref, up_ref, *refs, per_step, chunk
):
    images, (q_s, acc_ref, sums_ref, img_ref, up_s) = refs[:GROUPS], refs[GROUPS:]

    @pl.when(pl.program_id(0) == 0)
    def _():
        up = up_ref[0]
        none = jnp.zeros_like(up)
        up_s[:, :HD] = jnp.concatenate([up, none], axis=0)
        up_s[:, HD:] = jnp.concatenate([none, up], axis=0)

    rank = jnp.full((1, 2 * HD), rank_ref[here_ref[0]].astype(f32))
    acts = acts_ref[...].reshape(per_step * HALF, 2 * RANK)
    update = adapter_alpha / rank * jnp.dot(acts, up_s[...], preferred_element_type=f32)
    parts = [update[:, half * HD : (half + 1) * HD].reshape(per_step, HALF, HD) for half in range(2)]
    q = (q_ref[...].astype(f32) + jnp.concatenate(parts, axis=1)).astype(bf16)
    q_s[...] = q
    q = q.reshape(per_step * TOK, HD)

    acc, total = self_part(kv_ref, q, chunk)
    img_acc, img_total = image_part(images, q, chunk)
    acc_ref[0] = acc
    sums_ref[0, :8] = jnp.broadcast_to(total, (8, total.shape[1]))
    sums_ref[0, 8:] = jnp.zeros((8, total.shape[1]), f32)
    img_ref[0] = img_acc / img_total

    @pl.when(jnp.logical_not(in_range(total)))
    def _():
        acc, total, top = self_part_by_maximum(kv_ref, q_s[...].reshape(per_step * TOK, HD), chunk)
        acc_ref[0] = acc
        sums_ref[0, :8] = jnp.broadcast_to(total, (8, total.shape[1]))
        sums_ref[0, 8:] = jnp.broadcast_to(top, (8, total.shape[1]))

    @pl.when(jnp.logical_not(in_range(img_total)))
    def _():
        acc, total = image_part_by_maximum(images, q_s[...].reshape(per_step * TOK, HD))
        img_ref[0] = acc / total


def second_kernel(q_ref, kv_ref, acc_ref, sums_ref, img_ref, o_ref, *, per_step, chunk):
    q = q_ref[...].reshape(per_step * TOK, HD)

    def emit(acc, total, top):
        total1, top1 = sums_ref[0, :1], sums_ref[0, 8:9]
        both = jnp.maximum(top, top1)
        scale, scale1 = jnp.exp2(top - both), jnp.exp2(top1 - both)
        own = (acc * scale + acc_ref[0] * scale1) / (total * scale + total1 * scale1)
        out = own + ip_scale * img_ref[0]
        o_ref[...] = out.astype(bf16).T.reshape(per_step, TOK, HD)

    acc, total = self_part(kv_ref, q, chunk)
    emit(acc, total, jnp.zeros_like(total))

    @pl.when(jnp.logical_not(in_range(total)))
    def _():
        emit(*self_part_by_maximum(kv_ref, q_ref[...].reshape(per_step * TOK, HD), chunk))


PER_STEP, CHUNK = 4, 2048
STEPS = HEADS // PER_STEP
HEAD_BLOCK = pl.BlockSpec((PER_STEP, TOK, HD), lambda i: (i, 0, 0))
KEYS_BLOCK = pl.BlockSpec((HEADS, TOK, HD), lambda i: (0, 0, 0))
WIDE_BLOCK = pl.BlockSpec((1, HD, PER_STEP * TOK), lambda i: (i, 0, 0))
SUMS_BLOCK = pl.BlockSpec((1, 16, PER_STEP * TOK), lambda i: (i, 0, 0))


def attention_cost(keys):
    pairs = HEADS * TOK * keys
    return pl.CostEstimate(flops=pairs * HD * 4, bytes_accessed=8 << 20, transcendentals=pairs)


def attend_first(here, index, rank, first, adapters, images):
    def block(shape, at):
        return pl.BlockSpec(shape, lambda i, here, index, rank: at(i, here, index))

    each = lambda i, here, index: (i, 0, 0)
    image = block((CAP * IMG_TOK + FLAG_ROWS, 2 * HD), lambda i, here, index: (0, 0))
    wide = jax.ShapeDtypeStruct((STEPS, HD, PER_STEP * TOK), f32)
    return pl.pallas_call(
        functools.partial(first_kernel, per_step=PER_STEP, chunk=CHUNK),
        grid_spec=pltpu.PrefetchScalarGridSpec(
            num_scalar_prefetch=3,
            grid=(STEPS,),
            in_specs=[
                block((PER_STEP, TOK, HD), lambda i, here, index: (i, 1, 0)),
                block((PER_STEP, 2 * RANK, HD), lambda i, here, index: (i, 2 * TOK // (2 * RANK), 0)),
                block((HEADS, TOK, HD), lambda i, here, index: (0, 0, 0)),
                block((1, RANK, HD), lambda i, here, index: (holder(here, index), 0, WIDTH // HD)),
            ]
            + [image] * GROUPS,
            out_specs=[
                block((PER_STEP, TOK, HD), each),
                block((1, HD, PER_STEP * TOK), each),
                block((1, 16, PER_STEP * TOK), each),
                block((1, HD, PER_STEP * TOK), each),
            ],
            scratch_shapes=[pltpu.VMEM((2 * RANK, 2 * HD), bf16)],
        ),
        out_shape=[
            jax.ShapeDtypeStruct((HEADS, TOK, HD), bf16),
            wide,
            jax.ShapeDtypeStruct((STEPS, 16, PER_STEP * TOK), f32),
            wide,
        ],
        compiler_params=params(60),
        cost_estimate=attention_cost(HEADS * HALF + SLOTS * IMG_TOK),
    )(here, index, rank, first, first, first, adapters, *images)


def attend_second(updated, second, acc, sums, image):
    return pl.pallas_call(
        functools.partial(second_kernel, per_step=PER_STEP, chunk=CHUNK),
        grid=(STEPS,),
        in_specs=[HEAD_BLOCK, KEYS_BLOCK, WIDE_BLOCK, SUMS_BLOCK, WIDE_BLOCK],
        out_specs=HEAD_BLOCK,
        out_shape=jax.ShapeDtypeStruct((HEADS, TOK, HD), bf16),
        compiler_params=params(60),
        cost_estimate=attention_cost(HEADS * HALF),
    )(updated, second, acc, sums, image)


def along_x(k):
    return [(z * 4 + x, z * 4 + (x + k) % 4) for z in range(4) for x in range(4)]


def along_z(k):
    return [(z * 4 + x, ((z + k) % 4) * 4 + x) for z in range(4) for x in range(4)]


def along_req(k, d):
    return [(y * 2 + c, (y + k) % 4 * 2 + (c + d) % 2) for y in range(4) for c in range(2)]


def exchange(x):
    return lax.all_to_all(x, "sp", split_axis=0, concat_axis=0, tiled=True)


def after(x, *others):
    return lax.optimization_barrier((x,) + others)[0]


def shards(
    hidden,
    latent_query_key_value,
    features,
    image_request,
    image_key_weight,
    image_value_weight,
    caller_lowfactor_index,
    request_rank,
    lowfactor_reducing_matrix,
    lowfactor_expanding_matrix,
):
    here = lax.axis_index("req").reshape(1)
    place = lax.axis_index("sp").reshape(1)
    index, rank = caller_lowfactor_index, request_rank
    planes = latent_query_key_value[0].transpose(1, 0, 2)

    own = jnp.concatenate(
        [
            lowfactor_reducing_matrix.transpose(0, 2, 1),
            lax.dynamic_slice_in_dim(lowfactor_expanding_matrix, place[0] * HD, HD, 2),
        ],
        axis=2,
    )
    other = lax.ppermute(own, "req", along_req(0, 1))

    half = features.shape[0] // 2
    lines = []
    for part, way in ((features[:half], along_x), (features[half:], along_z)):
        line = [part] + [lax.ppermute(part, "sp", way(k)) for k in (1, 2, 3)]
        lines.append(jnp.stack(line).reshape(IMG_TOK, ENC))
    pieces = []
    for line, way in zip(lines, (along_z, along_x)):
        pieces += [line] + [lax.ppermute(line, "sp", way(k)) for k in (1, 2, 3)]

    chosen = choose_adapters(here, index, own, other)
    adapters = lax.all_to_all(
        chosen,
        "req",
        split_axis=0,
        concat_axis=0,
        tiled=True,
        axis_index_groups=[[y * 2 + core for y in range(4)] for core in range(2)],
    )

    packed = add_ranks(here, index, rank, hidden[0], adapters, pack_first(planes))
    first = exchange(after(packed, *pieces))

    ways = [(k, d) for k in range(4) for d in range(2)]
    placed = place_images(here, image_request[:, 0], pieces, image_key_weight, image_value_weight)
    images = [placed[0]] + [
        lax.ppermute(p, "req", along_req(k, d)) for p, (k, d) in zip(placed[1:], ways[1:])
    ]

    second = exchange(after(pack_second(planes), first, *images))
    updated, acc, sums, image = attend_first(here, index, rank, first, adapters, images)
    per_heads = attend_second(updated, second, acc, sums, image)
    return unpack_heads(exchange(per_heads))


def solution(mesh):
    placed = (
        P("req", "sp", None),
        P("req", "sp", None, None),
        P("req", "sp", None),
        P("req", None),
        P(None, "sp"),
        P(None, "sp"),
        P(),
        P(),
        P("req", None, None),
        P("req", None, None),
    )
    return jax.shard_map(
        shards, mesh=mesh, in_specs=placed, out_specs=P("req", "sp", None), check_vma=False
    )
```
